128 devices in a mesh: row: 8 (over x, core), col: 16 (over z, y).
Axes of the slice: x: 4, y: 4, z: 4, core: 2. Of those that a mesh axis runs over, the one named last changes fastest.
Arguments:
- panel: float32 [6, 2048, 2048], P(None, 'row', 'col'), may hold values from -0.0625 to 0.0625
- inverse_blocks: float32 [4, 2048, 2048], P(None, 'row', 'col'), may hold values from -1.5 to 1.5, as said below
- trailing_factor: float32 [12, 2048, 4, 2048], P(None, 'row', None, 'col'), may hold values from -0.0625 to 0.0625
- columns: float32 [4, 2048, 1024], P(None, 'row', 'col'), may hold values from -6 to 6
- trailing_columns: float32 [12, 2048, 1024], P(None, 'row', 'col'), may hold values from -6 to 6
Outputs:
- whitened: float32 [4, 2048, 1024], P(None, 'row', 'col')
- updated: float32 [12, 2048, 1024], P(None, 'row', 'col')
- variance_drop: float32 [1024], P('col')
The draws below stay inside these ranges and needn't reach their ends.
Inputs may be any that keep to these rules, and one draw needn't show every extreme that they name: `inverse_blocks`: each block is lower triangular; its diagonal entries lie between 0.5 and 1.5.
All inputs are finite; a program needn't handle non-finite values.
Results may differ from the reference program's by a relative error of at most 0.00011.
Values sent between devices are 32-bit elements; how exact they have to be, the bound alone decides.
No kernel may reach another device: no remote copies, remote signals or barrier semaphores. Data moves between devices by JAX's collectives and lax.ppermute only.
A program may use at most 128 MiB of HBM per device.

```python
import jax
import jax.numpy as jnp
from jax import lax

NB = 2048
STEPS = 4
TRAIL = 12
M = 1024
PAIRS = 6


def draw_inverse_blocks(key, part):
    key = jax.random.fold_in(key, 7)
    key_off, key_diag = jax.random.split(key)
    shape = (STEPS, NB, NB)
    rows = lax.broadcasted_iota(jnp.int32, shape, 1)
    cols = lax.broadcasted_iota(jnp.int32, shape, 2)
    off = jnp.clip(jax.random.normal(key_off, shape, jnp.float32), -6.0, 6.0) * (0.5 * NB ** (-0.5))
    diag = jax.random.uniform(key_diag, shape, jnp.float32, 0.5, 1.5)
    return jnp.where(rows == cols, diag, jnp.where(rows > cols, off, 0.0)).astype(jnp.float32)


def block_scale(key, shape, cuts, least, high):
    loudness, own = 1.0, jax.random.fold_in(key, 6)
    for axis_at, blocks in cuts:
        heights = jnp.exp(jax.random.uniform(jax.random.fold_in(own, axis_at), (blocks,), jnp.float32, least / len(cuts), high / len(cuts)))
        loudness = loudness * jnp.repeat(heights, shape[axis_at] // blocks).reshape([-1 if axis == axis_at else 1 for axis in range(len(shape))])
    return loudness


def scatter_about(own_key, shape, deviation, reach, shards=(), dtype=jnp.bfloat16):
    drawn = deviation * jax.random.normal(own_key, shape, jnp.float32)
    if shards:
        drawn = drawn * block_scale(own_key, shape, shards, -0.22, 0.18)
    return jnp.clip(drawn, -reach, reach).astype(dtype)


def setup_inputs(seed: int = 0) -> dict:
    key_of = jax.random.split(jax.random.key(seed), 6)
    return {
        "panel": scatter_about(key_of[0], (PAIRS, NB, NB), (4 * NB) ** -0.5, 0.0625, ((1, 8), (2, 16)), jnp.float32),
        "inverse_blocks": draw_inverse_blocks(jax.random.fold_in(key_of[5], 71), 0),
        "trailing_factor": scatter_about(key_of[2], (TRAIL, NB, STEPS, NB), (4 * NB) ** -0.5, 0.0625, ((1, 8), (3, 16)), jnp.float32),
        "columns": scatter_about(key_of[3], (STEPS, NB, M), 1.0, 6.0, ((1, 8), (2, 16)), jnp.float32),
        "trailing_columns": scatter_about(key_of[4], (TRAIL, NB, M), 1.0, 6.0, ((1, 8), (2, 16)), jnp.float32),
    }


def product(left, right):
    return jnp.dot(left, right, precision=lax.Precision.HIGHEST, preferred_element_type=jnp.float32)


def reference(panel, inverse_blocks, trailing_factor, columns, trailing_columns):
    solved = []
    for j in range(STEPS):
        reduced = columns[j]
        if j > 0:
            total = jnp.zeros_like(reduced)
            for i in range(j):
                total = total + product(panel[j * (j - 1) // 2 + i], solved[i])
            reduced = reduced - total
        solved.append(product(inverse_blocks[j], reduced))
    whitened = jnp.stack(solved)

    def trail_row(pair):
        factor_row, column_row = pair
        acc = jnp.zeros_like(column_row)
        for j in range(STEPS):
            acc = acc + product(factor_row[:, j, :], whitened[j])
        return column_row - acc

    updated = lax.map(trail_row, (trailing_factor, trailing_columns))
    variance_drop = jnp.sum(whitened * whitened, axis=(0, 1)) / (STEPS * NB)
    return whitened, updated, variance_drop
```

```python
import jax
import jax.numpy as jnp
import numpy as np
from jax import lax
from jax.experimental import pallas as pl
from jax.experimental.pallas import tpu as pltpu
from jax.sharding import Mesh, PartitionSpec as P

ROW, COL = ("x", "core"), ("z", "y")
ALL = ROW + COL
NT = (((1,), (1,)), ((), ()))
RING = {s: [(i, (i + s) % 4) for i in range(4)] for s in (1, 2, 3)}
SWAP = [(0, 1), (1, 0)]
LOCAL = pl.BlockSpec(memory_space=pltpu.VMEM)


def both_cores(pieces):
    return pieces + [lax.ppermute(piece, "core", SWAP) for piece in pieces]


def row_gather(block):
    return both_cores([block] + [lax.ppermute(block, "x", RING[s]) for s in (1, 2, 3)])


def turned(s):
    pairs = []
    for a in range(4):
        for core in range(2):
            for b in range(4):
                for y in range(4):
                    source = ((a * 2 + core) * 4 + b) * 4 + y
                    target = ((((b - s) % 4) * 2 + core) * 4 + a) * 4 + y
                    pairs.append((source, target))
    return pairs


def slab_gather(block):
    return both_cores([lax.ppermute(block, ALL, turned(s)) for s in range(4)])


def y_gather(blocks):
    return [blocks] + [lax.ppermute(blocks, "y", RING[s]) for s in (1, 2, 3)]


def z_sum(parts):
    total = parts[0]
    for t in (1, 2, 3):
        total = total + lax.ppermute(parts[t], "z", RING[t])
    return total


def split(v):
    high = v.astype(jnp.bfloat16)
    return high, (v - high.astype(jnp.float32)).astype(jnp.bfloat16)


def three(v, doubled):
    high, low = split(v)
    return jnp.concatenate([high, high, low] if doubled else [high, low, high], axis=1)


def local_call(kernel, operands, shapes, scratch, name, flops):
    nbytes = 4 * sum(int(np.prod(v.shape)) for v in operands)
    return pl.pallas_call(
        kernel,
        out_shape=shapes,
        in_specs=[LOCAL] * len(operands),
        out_specs=jax.tree.map(lambda _: LOCAL, shapes),
        scratch_shapes=scratch,
        cost_estimate=pl.CostEstimate(flops=flops, bytes_accessed=nbytes, transcendentals=0),
        name=name,
    )(*operands)


def slab_product(factor, indices, gathered):
    n = len(indices)

    def kernel(*refs):
        f, pieces, out, (chunks, blocks) = refs[:4], refs[4:12], refs[12:16], refs[16:]
        x, z, y, core = (lax.axis_index(name) for name in ("x", "z", "y", "core"))
        for side, which in ((0, core), (4, 1 - core)):
            for h in range(2):
                for s in range(4):
                    chunks[which * 2 + h, s * 64 : s * 64 + 64] = pieces[side + s][:, h * 128 : h * 128 + 128]
        for at, index in enumerate(indices):
            value = jnp.zeros((256, 256), jnp.float32)
            for k in (0, 2):
                rows = jnp.concatenate([chunks[lax.rem(y - k - h + 4, 4)] for h in (0, 1)], axis=1)
                block = jnp.concatenate([f[k][index], f[k + 1][index]], axis=1)
                value += lax.dot_general(three(rows, False), three(block, True), NT, preferred_element_type=jnp.float32)
            blocks[at] = value.reshape(4, 64, 256)
        for t in range(4):
            for at in range(n):
                out[t][at] = blocks[at, lax.rem(t + z - x + 4, 4)]

    return local_call(
        kernel,
        [*factor, *gathered],
        [jax.ShapeDtypeStruct((n, 64, 256), jnp.float32)] * 4,
        [pltpu.VMEM((4, 256, 128), jnp.float32), pltpu.VMEM((n, 4, 64, 256), jnp.float32)],
        "slab_product",
        n * 2 * 3 * 256 * 256 * 512,
    )


def by_row(pieces):
    x, core = lax.axis_index("x"), lax.axis_index("core")
    for side, which in ((0, core), (4, 1 - core)):
        for k in range(4):
            yield lax.rem(x - k + 4, 4) * 2 + which, pieces[side + k]


def full_product(base, terms):
    n = len(terms)

    def kernel(*refs):
        scratch = refs[len(refs) - n :]
        out = refs[len(refs) - n - 1]
        both = jnp.zeros((128, 256), jnp.float32)
        cross = jnp.zeros((64, 256), jnp.float32)
        for term, chunks in enumerate(scratch):
            f, pieces = refs[9 * term], refs[9 * term + 1 : 9 * term + 9]
            for row, piece in by_row(pieces):
                chunks[row, :64], chunks[row, 64:] = split(piece[...])
            for q in range(8):
                high, low = split(jnp.concatenate([f[2 * q], f[2 * q + 1]], axis=1))
                rows = chunks[q]
                both += lax.dot_general(rows, high, NT, preferred_element_type=jnp.float32)
                cross += lax.dot_general(rows[:64], low, NT, preferred_element_type=jnp.float32)
        total = both[:64] + both[64:] + cross
        out[...] = total if base is None else refs[9 * n][...] - total

    operands = [v for block, gathered in terms for v in (block, *gathered)]
    return local_call(
        kernel,
        operands + ([] if base is None else [base]),
        jax.ShapeDtypeStruct((64, 256), jnp.float32),
        [pltpu.VMEM((8, 128, 256), jnp.bfloat16)] * n,
        "full_product",
        n * 2 * 3 * 64 * 256 * 2048,
    )


def spread_to(turn):
    return [(r * 16 + 2 * q + b, q * 16 + 2 * r + (b + turn) % 2) for r in range(8) for q in range(8) for b in range(2)]


def spread(blocks):
    n = blocks.shape[0]
    odd = lax.axis_index("y") % 2 == 1
    low, high = blocks[:, :, :128], blocks[:, :, 128:]
    same = lax.ppermute(jnp.where(odd, high, low), ALL, spread_to(0))
    cross = lax.ppermute(jnp.where(odd, low, high), ALL, spread_to(1))
    gathered = row_gather(jnp.concatenate([jnp.where(odd, cross, same), jnp.where(odd, same, cross)], axis=1))

    def kernel(*refs):
        out = refs[-1]
        for row, piece in by_row(refs[:8]):
            at = pl.ds(pl.multiple_of(row * 128, 128), 128)
            for j in range(n):
                one, two = split(piece[j])
                out[at, j * 128 : j * 128 + 128] = one
                out[at, (n + j) * 128 : (n + j + 1) * 128] = two

    return local_call(kernel, gathered, jax.ShapeDtypeStruct((1024, 2 * n * 128), jnp.bfloat16), [], "split_rows", 0)


def trailing_product(factor, early, last):
    def kernel(f, early, last, out, rows):
        @pl.when(pl.program_id(0) == 0)
        def _():
            for part, side in enumerate((0, 1, 0)):
                rows[:, part * 512 : part * 512 + 384] = early[:, side * 384 : side * 384 + 384]
                rows[:, part * 512 + 384 : part * 512 + 512] = last[:, side * 128 : side * 128 + 128]

        block = jnp.concatenate([f[0, pl.ds(j, 256, stride=4), :] for j in range(4)], axis=1)
        value = lax.dot_general(rows[...], three(block, True), NT, preferred_element_type=jnp.float32)
        out[:, 0] = value.reshape(16, 64, 256)

    return pl.pallas_call(
        kernel,
        grid=(12,),
        out_shape=jax.ShapeDtypeStruct((16, 12, 64, 256), jnp.float32),
        in_specs=[
            pl.BlockSpec((1, 1024, 128), lambda t: (t, 0, 0)),
            pl.BlockSpec((1024, 768), lambda t: (0, 0)),
            pl.BlockSpec((1024, 256), lambda t: (0, 0)),
        ],
        out_specs=pl.BlockSpec((16, 1, 64, 256), lambda t: (0, t, 0, 0)),
        scratch_shapes=[pltpu.VMEM((1024, 1536), jnp.bfloat16)],
        compiler_params=pltpu.CompilerParams(vmem_limit_bytes=56 * 1024 * 1024),
        cost_estimate=pl.CostEstimate(flops=2 * 3 * 1024 * 3072 * 512, bytes_accessed=20971520, transcendentals=0),
        name="trailing_product",
    )(factor, early, last)


def shards(panel, inverse_blocks, trailing_factor, columns, trailing_columns):
    columns_t = jnp.transpose(columns, (0, 2, 1))
    group = y_gather(jnp.concatenate([inverse_blocks[0:1], panel[1:2], panel[3:4]]))
    near = lax.all_gather(jnp.concatenate([panel[0:1], inverse_blocks[1:2], panel[2:3], inverse_blocks[2:3]]), COL, axis=0)
    far = lax.all_gather(jnp.concatenate([panel[4:6], inverse_blocks[3:4]]), COL, axis=0)

    first = z_sum(slab_product(group, (0,), slab_gather(columns_t[0])))[0]
    gathered = row_gather(first)
    later, gathered = lax.optimization_barrier((first, gathered))
    parts = slab_product(group, (1, 2), slab_gather(later))
    near, parts = lax.optimization_barrier((near, parts))
    bases = columns_t[2:4] - z_sum(parts)

    reduced = full_product(columns_t[1], [(near[:, 0], gathered)])
    second = full_product(None, [(near[:, 1], row_gather(reduced))])
    gathered_second = row_gather(second)
    reduced = full_product(bases[0], [(near[:, 2], gathered_second)])
    third = full_product(None, [(near[:, 3], row_gather(reduced))])
    gathered = row_gather(third)
    (first, second, third), gathered = lax.optimization_barrier(((first, second, third), gathered))
    early = spread(jnp.stack([first, second, third]))
    reduced = full_product(bases[1], [(far[:, 0], gathered_second), (far[:, 1], gathered)])
    fourth = full_product(None, [(far[:, 2], row_gather(reduced))])

    partial = trailing_product(trailing_factor.reshape(12, 1024, 128), early, spread(fourth[None]))
    updated = jnp.transpose(trailing_columns, (0, 2, 1)) - lax.psum_scatter(partial, COL, scatter_dimension=0)

    whitened_t = jnp.stack([first, second, third, fourth])
    local_squares = jnp.sum(whitened_t * whitened_t, axis=(0, 2))
    variance_drop = lax.psum(local_squares, ROW) / 8192
    return (jnp.transpose(whitened_t, (0, 2, 1)), jnp.transpose(updated, (0, 2, 1)), variance_drop)


def solution(mesh):
    mesh = Mesh(np.asarray(mesh.devices).reshape(4, 2, 4, 4), ("x", "core", "z", "y"))
    return jax.shard_map(
        shards,
        mesh=mesh,
        in_specs=(
            P(None, ROW, COL),
            P(None, ROW, COL),
            P(None, ROW, None, COL),
            P(None, ROW, COL),
            P(None, ROW, COL),
        ),
        out_specs=(P(None, ROW, COL), P(None, ROW, COL), P(COL)),
        check_vma=False,
    )
```

```python
import jax
import jax.numpy as jnp
import numpy as np
from jax import lax
from jax.experimental import pallas as pl
from jax.experimental.pallas import tpu as pltpu
from jax.sharding import Mesh, PartitionSpec as P

ROW, COL = ("x", "core"), ("z", "y")
ALL = ROW + COL
NT = (((1,), (1,)), ((), ()))
RING = {s: [(i, (i + s) % 4) for i in range(4)] for s in (1, 2, 3)}
SWAP = [(0, 1), (1, 0)]
LOCAL = pl.BlockSpec(memory_space=pltpu.VMEM)


def both_cores(pieces):
    return pieces + [lax.ppermute(piece, "core", SWAP) for piece in pieces]


def row_gather(block):
    return both_cores([block] + [lax.ppermute(block, "x", RING[s]) for s in (1, 2, 3)])


def turned(s):
    pairs = []
    for a in range(4):
        for core in range(2):
            for b in range(4):
                for y in range(4):
                    source = ((a * 2 + core) * 4 + b) * 4 + y
                    target = ((((b - s) % 4) * 2 + core) * 4 + a) * 4 + y
                    pairs.append((source, target))
    return pairs


def slab_gather(block):
    return both_cores([lax.ppermute(block, ALL, turned(s)) for s in range(4)])


def y_gather(blocks):
    return [blocks] + [lax.ppermute(blocks, "y", RING[s]) for s in (1, 2, 3)]


def z_sum(parts):
    total = parts[0]
    for t in (1, 2, 3):
        total = total + lax.ppermute(parts[t], "z", RING[t])
    return total


def split(v):
    high = v.astype(jnp.bfloat16)
    return high, (v - high.astype(jnp.float32)).astype(jnp.bfloat16)


def three(v, doubled):
    high, low = split(v)
    return jnp.concatenate([high, high, low] if doubled else [high, low, high], axis=1)


def in_vmem(shape, dtype=jnp.float32):
    return pltpu.VMEM(shape, dtype)


def local_call(kernel, operands, shapes, scratch, name, flops):
    nbytes = 4 * sum(int(np.prod(v.shape)) for v in operands)
    return pl.pallas_call(
        kernel,
        out_shape=shapes,
        in_specs=[LOCAL] * len(operands),
        out_specs=[LOCAL] * len(shapes) if isinstance(shapes, list) else LOCAL,
        scratch_shapes=scratch,
        compiler_params=pltpu.CompilerParams(vmem_limit_bytes=16 * 1024 * 1024),
        cost_estimate=pl.CostEstimate(flops=flops, bytes_accessed=nbytes, transcendentals=0),
        name=name,
    )(*[pltpu.with_memory_space_constraint(v, pltpu.VMEM) for v in operands])


def fetch(blocks, index):
    def kernel(blocks_ref, out, sem):
        copy = pltpu.make_async_copy(blocks_ref.at[:, index], out, sem)
        copy.start()
        copy.wait()

    return pl.pallas_call(
        kernel,
        out_shape=in_vmem((16, 256, 128)),
        in_specs=[pl.BlockSpec(memory_space=pl.ANY)],
        out_specs=LOCAL,
        scratch_shapes=[pltpu.SemaphoreType.DMA],
        compiler_params=pltpu.CompilerParams(vmem_limit_bytes=8 * 1024 * 1024),
        cost_estimate=pl.CostEstimate(flops=0, bytes_accessed=4194304, transcendentals=0),
        name="fetch",
    )(blocks)


def slab_product(factor, indices, gathered):
    n = len(indices)

    def kernel(*refs):
        f, pieces, out, (chunks, blocks) = refs[:4], refs[4:12], refs[12:16], refs[16:]
        x, z, y, core = (lax.axis_index(name) for name in ("x", "z", "y", "core"))
        for side, which in ((0, core), (4, 1 - core)):
            for h in range(2):
                for s in range(4):
                    chunks[which * 2 + h, s * 64 : s * 64 + 64] = pieces[side + s][:, h * 128 : h * 128 + 128]
        for at, index in enumerate(indices):
            value = jnp.zeros((256, 256), jnp.float32)
            for k in (0, 2):
                rows = jnp.concatenate([chunks[lax.rem(y - k - h + 4, 4)] for h in (0, 1)], axis=1)
                block = jnp.concatenate([f[k][index], f[k + 1][index]], axis=1)
                value += lax.dot_general(three(rows, False), three(block, True), NT, preferred_element_type=jnp.float32)
            blocks[at] = value.reshape(4, 64, 256)
        for t in range(4):
            for at in range(n):
                out[t][at] = blocks[at, lax.rem(t + z - x + 4, 4)]

    return local_call(
        kernel,
        [*factor, *gathered],
        [in_vmem((n, 64, 256))] * 4,
        [pltpu.VMEM((4, 256, 128), jnp.float32), pltpu.VMEM((n, 4, 64, 256), jnp.float32)],
        "slab_product",
        n * 2 * 3 * 256 * 256 * 512,
    )


def by_row(pieces):
    x, core = lax.axis_index("x"), lax.axis_index("core")
    for side, which in ((0, core), (4, 1 - core)):
        for k in range(4):
            yield lax.rem(x - k + 4, 4) * 2 + which, pieces[side + k]


def full_product(base, terms):
    n = len(terms)

    def kernel(*refs):
        scratch = refs[len(refs) - n :]
        out = refs[len(refs) - n - 1]
        both = jnp.zeros((128, 256), jnp.float32)
        cross = jnp.zeros((64, 256), jnp.float32)
        for term, chunks in enumerate(scratch):
            f, pieces = refs[9 * term], refs[9 * term + 1 : 9 * term + 9]
            for row, piece in by_row(pieces):
                chunks[row, :64], chunks[row, 64:] = split(piece[...])
            for q in range(8):
                high, low = split(jnp.concatenate([f[2 * q], f[2 * q + 1]], axis=1))
                rows = chunks[q]
                both += lax.dot_general(rows, high, NT, preferred_element_type=jnp.float32)
                cross += lax.dot_general(rows[:64], low, NT, preferred_element_type=jnp.float32)
        total = both[:64] + both[64:] + cross
        out[...] = total if base is None else refs[9 * n][...] - total

    operands = [v for block, gathered in terms for v in (block, *gathered)]
    return local_call(
        kernel,
        operands + ([] if base is None else [base]),
        in_vmem((64, 256)),
        [pltpu.VMEM((8, 128, 256), jnp.bfloat16)] * n,
        "full_product",
        n * 2 * 3 * 64 * 256 * 2048,
    )


def spread_to(turn):
    return [(r * 16 + 2 * q + b, q * 16 + 2 * r + (b + turn) % 2) for r in range(8) for q in range(8) for b in range(2)]


def spread(blocks):
    n = blocks.shape[0]
    odd = lax.axis_index("y") % 2 == 1
    low, high = blocks[:, :, :128], blocks[:, :, 128:]
    same = lax.ppermute(jnp.where(odd, high, low), ALL, spread_to(0))
    cross = lax.ppermute(jnp.where(odd, low, high), ALL, spread_to(1))
    gathered = row_gather(jnp.concatenate([jnp.where(odd, cross, same), jnp.where(odd, same, cross)], axis=1))

    def kernel(*refs):
        out = refs[-1]
        for row, piece in by_row(refs[:8]):
            at = pl.ds(pl.multiple_of(row * 128, 128), 128)
            for j in range(n):
                one, two = split(piece[j])
                out[at, j * 128 : j * 128 + 128] = one
                out[at, (n + j) * 128 : (n + j + 1) * 128] = two

    return local_call(kernel, gathered, in_vmem((1024, 2 * n * 128), jnp.bfloat16), [], "split_rows", 0)


def trailing_product(factor, early, last):
    def kernel(f, early, last, out, rows):
        @pl.when(pl.program_id(0) == 0)
        def _():
            for part, side in enumerate((0, 1, 0)):
                rows[:, part * 512 : part * 512 + 384] = early[:, side * 384 : side * 384 + 384]
                rows[:, part * 512 + 384 : part * 512 + 512] = last[:, side * 128 : side * 128 + 128]

        block = jnp.concatenate([f[0, pl.ds(j, 256, stride=4), :] for j in range(4)], axis=1)
        value = lax.dot_general(rows[...], three(block, True), NT, preferred_element_type=jnp.float32)
        out[:, 0] = value.reshape(16, 64, 256)

    return pl.pallas_call(
        kernel,
        grid=(12,),
        out_shape=jax.ShapeDtypeStruct((16, 12, 64, 256), jnp.float32),
        in_specs=[
            pl.BlockSpec((1, 1024, 128), lambda t: (t, 0, 0)),
            pl.BlockSpec((1024, 768), lambda t: (0, 0)),
            pl.BlockSpec((1024, 256), lambda t: (0, 0)),
        ],
        out_specs=pl.BlockSpec((16, 1, 64, 256), lambda t: (0, t, 0, 0)),
        scratch_shapes=[pltpu.VMEM((1024, 1536), jnp.bfloat16)],
        compiler_params=pltpu.CompilerParams(vmem_limit_bytes=56 * 1024 * 1024),
        cost_estimate=pl.CostEstimate(flops=2 * 3 * 1024 * 3072 * 512, bytes_accessed=20971520, transcendentals=0),
        name="trailing_product",
    )(factor, early, last)


def shards(panel, inverse_blocks, trailing_factor, columns, trailing_columns):
    columns_t = jnp.transpose(columns, (0, 2, 1))
    group = y_gather(inverse_blocks[0:1])
    below = y_gather(jnp.concatenate([panel[0:2], panel[3:4]]))
    near = lax.all_gather(jnp.concatenate([inverse_blocks[1:2], panel[2:3], inverse_blocks[2:3]]), COL, axis=0)
    far = lax.all_gather(jnp.concatenate([panel[4:6], inverse_blocks[3:4]]), COL, axis=0)

    first = z_sum(slab_product(group, (0,), slab_gather(columns_t[0])))[0]
    bases = columns_t[1:4] - z_sum(slab_product(below, (0, 1, 2), slab_gather(first)))
    second = full_product(None, [(fetch(near, 0), row_gather(bases[0]))])
    gathered_second = row_gather(second)
    reduced = full_product(bases[1], [(fetch(near, 1), gathered_second)])
    third = full_product(None, [(fetch(near, 2), row_gather(reduced))])
    gathered = row_gather(third)
    (first, second, third), gathered = lax.optimization_barrier(((first, second, third), gathered))
    early = spread(jnp.stack([first, second, third]))
    early, far = lax.optimization_barrier((early, far))
    reduced = full_product(bases[2], [(fetch(far, 0), gathered_second), (fetch(far, 1), gathered)])
    fourth = full_product(None, [(fetch(far, 2), row_gather(reduced))])

    partial = trailing_product(trailing_factor.reshape(12, 1024, 128), early, spread(fourth[None]))
    updated = jnp.transpose(trailing_columns, (0, 2, 1)) - lax.psum_scatter(partial, COL, scatter_dimension=0)

    whitened_t = jnp.stack([first, second, third, fourth])
    local_squares = jnp.sum(whitened_t * whitened_t, axis=(0, 2))
    variance_drop = lax.psum(local_squares, ROW) / 8192
    return (jnp.transpose(whitened_t, (0, 2, 1)), jnp.transpose(updated, (0, 2, 1)), variance_drop)


def solution(mesh):
    mesh = Mesh(np.asarray(mesh.devices).reshape(4, 2, 4, 4), ("x", "core", "z", "y"))
    return jax.shard_map(
        shards,
        mesh=mesh,
        in_specs=(
            P(None, ROW, COL),
            P(None, ROW, COL),
            P(None, ROW, None, COL),
            P(None, ROW, COL),
            P(None, ROW, COL),
        ),
        out_specs=(P(None, ROW, COL), P(None, ROW, COL), P(COL)),
        check_vma=False,
    )
```

```python
import jax
import jax.numpy as jnp
import numpy as np
from jax import lax
from jax.experimental import pallas as pl
from jax.experimental.pallas import tpu as pltpu
from jax.sharding import Mesh, PartitionSpec as P

ROW, COL = ("x", "core"), ("z", "y")
ALL = ROW + COL
NT = (((1,), (1,)), ((), ()))
RING = {s: [(i, (i + s) % 4) for i in range(4)] for s in (1, 2, 3)}
SWAP = [(0, 1), (1, 0)]
LOCAL = pl.BlockSpec(memory_space=pltpu.VMEM)


def both_cores(pieces):
    return pieces + [lax.ppermute(piece, "core", SWAP) for piece in pieces]


def row_gather(block):
    return both_cores([block] + [lax.ppermute(block, "x", RING[s]) for s in (1, 2, 3)])


def row_gather_beside(block, beside):
    pieces = [block] + [lax.ppermute(block, "x", RING[s]) for s in (1, 2, 3)]
    own, beside = lax.optimization_barrier((block, beside))
    return pieces + [lax.ppermute(piece, "core", SWAP) for piece in [own] + pieces[1:]], beside


def turned(s):
    pairs = []
    for a in range(4):
        for core in range(2):
            for b in range(4):
                for y in range(4):
                    source = ((a * 2 + core) * 4 + b) * 4 + y
                    target = ((((b - s) % 4) * 2 + core) * 4 + a) * 4 + y
                    pairs.append((source, target))
    return pairs


def slab_gather(block):
    return both_cores([lax.ppermute(block, ALL, turned(s)) for s in range(4)])


def y_gather(blocks):
    return [blocks] + [lax.ppermute(blocks, "y", RING[s]) for s in (1, 2, 3)]


def z_sum(parts):
    total = parts[0]
    for t in (1, 2, 3):
        total = total + lax.ppermute(parts[t], "z", RING[t])
    return total


def split(v):
    high = v.astype(jnp.bfloat16)
    return high, (v - high.astype(jnp.float32)).astype(jnp.bfloat16)


def three(v, doubled):
    high, low = split(v)
    return jnp.concatenate([high, high, low] if doubled else [high, low, high], axis=1)


def in_vmem(shape, dtype=jnp.float32):
    return pltpu.VMEM(shape, dtype)


def local_call(kernel, operands, shapes, scratch, name, flops):
    nbytes = 4 * sum(int(np.prod(v.shape)) for v in operands)
    return pl.pallas_call(
        kernel,
        out_shape=shapes,
        in_specs=[LOCAL] * len(operands),
        out_specs=[LOCAL] * len(shapes) if isinstance(shapes, list) else LOCAL,
        scratch_shapes=scratch,
        compiler_params=pltpu.CompilerParams(vmem_limit_bytes=16 * 1024 * 1024),
        cost_estimate=pl.CostEstimate(flops=flops, bytes_accessed=nbytes, transcendentals=0),
        name=name,
    )(*[pltpu.with_memory_space_constraint(v, pltpu.VMEM) for v in operands])


def fetch(blocks, index):
    def kernel(blocks_ref, out, sems):
        copies = []
        for i in range(4):
            part = pl.ds(4 * i, 4)
            copies.append(pltpu.make_async_copy(blocks_ref.at[part, index], out.at[part], sems.at[i]))
        for copy in copies:
            copy.start()
        for copy in copies:
            copy.wait()

    return pl.pallas_call(
        kernel,
        out_shape=in_vmem((16, 256, 128)),
        in_specs=[pl.BlockSpec(memory_space=pl.ANY)],
        out_specs=LOCAL,
        scratch_shapes=[pltpu.SemaphoreType.DMA((4,))],
        compiler_params=pltpu.CompilerParams(vmem_limit_bytes=8 * 1024 * 1024),
        cost_estimate=pl.CostEstimate(flops=0, bytes_accessed=4194304, transcendentals=0),
        name="fetch",
    )(pltpu.with_memory_space_constraint(blocks, pltpu.HBM))


def slab_product(factor, indices, gathered):
    n = len(indices)

    def kernel(*refs):
        f, pieces, out, (chunks, blocks) = refs[:4], refs[4:12], refs[12:16], refs[16:]
        x, z, y, core = (lax.axis_index(name) for name in ("x", "z", "y", "core"))
        for side, which in ((0, core), (4, 1 - core)):
            for h in range(2):
                for s in range(4):
                    chunks[which * 2 + h, s * 64 : s * 64 + 64] = pieces[side + s][:, h * 128 : h * 128 + 128]
        for at, index in enumerate(indices):
            value = jnp.zeros((256, 256), jnp.float32)
            for k in (0, 2):
                rows = jnp.concatenate([chunks[lax.rem(y - k - h + 4, 4)] for h in (0, 1)], axis=1)
                block = jnp.concatenate([f[k][index], f[k + 1][index]], axis=1)
                value += lax.dot_general(three(rows, False), three(block, True), NT, preferred_element_type=jnp.float32)
            blocks[at] = value.reshape(4, 64, 256)
        for t in range(4):
            for at in range(n):
                out[t][at] = blocks[at, lax.rem(t + z - x + 4, 4)]

    return local_call(
        kernel,
        [*factor, *gathered],
        [in_vmem((n, 64, 256))] * 4,
        [pltpu.VMEM((4, 256, 128), jnp.float32), pltpu.VMEM((n, 4, 64, 256), jnp.float32)],
        "slab_product",
        n * 2 * 3 * 256 * 256 * 512,
    )


def by_row(pieces):
    x, core = lax.axis_index("x"), lax.axis_index("core")
    for side, which in ((0, core), (4, 1 - core)):
        for k in range(4):
            yield lax.rem(x - k + 4, 4) * 2 + which, pieces[side + k]


def full_product(base, terms):
    n = len(terms)

    def kernel(*refs):
        scratch = refs[len(refs) - n :]
        out = refs[len(refs) - n - 1]
        both = jnp.zeros((128, 256), jnp.float32)
        cross = jnp.zeros((64, 256), jnp.float32)
        for term, chunks in enumerate(scratch):
            f, pieces = refs[9 * term], refs[9 * term + 1 : 9 * term + 9]
            for row, piece in by_row(pieces):
                chunks[row, :64], chunks[row, 64:] = split(piece[...])
            for q in range(8):
                high, low = split(jnp.concatenate([f[2 * q], f[2 * q + 1]], axis=1))
                rows = chunks[q]
                both += lax.dot_general(rows, high, NT, preferred_element_type=jnp.float32)
                cross += lax.dot_general(rows[:64], low, NT, preferred_element_type=jnp.float32)
        total = both[:64] + both[64:] + cross
        out[...] = total if base is None else refs[9 * n][...] - total

    operands = [v for block, gathered in terms for v in (block, *gathered)]
    return local_call(
        kernel,
        operands + ([] if base is None else [base]),
        in_vmem((64, 256)),
        [pltpu.VMEM((8, 128, 256), jnp.bfloat16)] * n,
        "full_product",
        n * 2 * 3 * 64 * 256 * 2048,
    )


def spread_to(turn):
    return [(r * 16 + 2 * q + b, q * 16 + 2 * r + (b + turn) % 2) for r in range(8) for q in range(8) for b in range(2)]


def spread(blocks):
    n = blocks.shape[0]
    odd = lax.axis_index("y") % 2 == 1
    low, high = blocks[:, :, :128], blocks[:, :, 128:]
    same = lax.ppermute(jnp.where(odd, high, low), ALL, spread_to(0))
    cross = lax.ppermute(jnp.where(odd, low, high), ALL, spread_to(1))
    gathered = row_gather(jnp.concatenate([jnp.where(odd, cross, same), jnp.where(odd, same, cross)], axis=1))

    def kernel(*refs):
        out = refs[-1]
        for row, piece in by_row(refs[:8]):
            at = pl.ds(pl.multiple_of(row * 128, 128), 128)
            for j in range(n):
                one, two = split(piece[j])
                out[at, j * 128 : j * 128 + 128] = one
                out[at, (n + j) * 128 : (n + j + 1) * 128] = two

    return local_call(kernel, gathered, in_vmem((1024, 2 * n * 128), jnp.bfloat16), [], "split_rows", 0)


def trailing_product(factor, early, last):
    def kernel(f, early, last, out, rows):
        @pl.when(pl.program_id(0) == 0)
        def _():
            for part, side in enumerate((0, 1, 0)):
                rows[:, part * 512 : part * 512 + 384] = early[:, side * 384 : side * 384 + 384]
                rows[:, part * 512 + 384 : part * 512 + 512] = last[:, side * 128 : side * 128 + 128]

        for t in range(2):
            block = jnp.concatenate([f[t, pl.ds(j, 256, stride=4), :] for j in range(4)], axis=1)
            value = lax.dot_general(rows[...], three(block, True), NT, preferred_element_type=jnp.float32)
            out[:, t] = value.reshape(16, 64, 256)

    return pl.pallas_call(
        kernel,
        grid=(6,),
        out_shape=jax.ShapeDtypeStruct((16, 12, 64, 256), jnp.float32),
        in_specs=[
            pl.BlockSpec((2, 1024, 128), lambda t: (t, 0, 0)),
            pl.BlockSpec((1024, 768), lambda t: (0, 0)),
            pl.BlockSpec((1024, 256), lambda t: (0, 0)),
        ],
        out_specs=pl.BlockSpec((16, 2, 64, 256), lambda t: (0, t, 0, 0)),
        scratch_shapes=[pltpu.VMEM((1024, 1536), jnp.bfloat16)],
        compiler_params=pltpu.CompilerParams(vmem_limit_bytes=56 * 1024 * 1024),
        cost_estimate=pl.CostEstimate(flops=2 * 3 * 1024 * 3072 * 512, bytes_accessed=20971520, transcendentals=0),
        name="trailing_product",
    )(factor, early, last)


def shards(panel, inverse_blocks, trailing_factor, columns, trailing_columns):
    columns_t = jnp.transpose(columns, (0, 2, 1))
    group = y_gather(inverse_blocks[0:1])
    below = y_gather(jnp.concatenate([panel[0:2], panel[3:4]]))
    near = lax.all_gather(jnp.concatenate([inverse_blocks[1:2], panel[2:3], inverse_blocks[2:3]]), COL, axis=0)
    far = lax.all_gather(jnp.concatenate([panel[4:6], inverse_blocks[3:4]]), COL, axis=0)

    first = z_sum(slab_product(group, (0,), slab_gather(columns_t[0])))[0]
    bases = columns_t[1:4] - z_sum(slab_product(below, (0, 1, 2), slab_gather(first)))
    second = full_product(None, [(fetch(near, 0), row_gather(bases[0]))])
    gathered_second, block = row_gather_beside(second, fetch(near, 1))
    reduced = full_product(bases[1], [(block, gathered_second)])
    gathered, block = row_gather_beside(reduced, fetch(near, 2))
    third = full_product(None, [(block, gathered)])
    gathered = row_gather(third)
    (first, second, third), gathered = lax.optimization_barrier(((first, second, third), gathered))
    early = spread(jnp.stack([first, second, third]))
    early, far = lax.optimization_barrier((early, far))
    reduced = full_product(bases[2], [(fetch(far, 0), gathered_second), (fetch(far, 1), gathered)])
    gathered, block = row_gather_beside(reduced, fetch(far, 2))
    fourth = full_product(None, [(block, gathered)])

    partial = trailing_product(trailing_factor.reshape(12, 1024, 128), early, spread(fourth[None]))
    updated = jnp.transpose(trailing_columns, (0, 2, 1)) - lax.psum_scatter(partial, COL, scatter_dimension=0)

    whitened_t = jnp.stack([first, second, third, fourth])
    local_squares = jnp.sum(whitened_t * whitened_t, axis=(0, 2))
    variance_drop = lax.psum(local_squares, ROW) / 8192
    return (jnp.transpose(whitened_t, (0, 2, 1)), jnp.transpose(updated, (0, 2, 1)), variance_drop)


def solution(mesh):
    mesh = Mesh(np.asarray(mesh.devices).reshape(4, 2, 4, 4), ("x", "core", "z", "y"))
    return jax.shard_map(
        shards,
        mesh=mesh,
        in_specs=(
            P(None, ROW, COL),
            P(None, ROW, COL),
            P(None, ROW, None, COL),
            P(None, ROW, COL),
            P(None, ROW, COL),
        ),
        out_specs=(P(None, ROW, COL), P(None, ROW, COL), P(COL)),
        check_vma=False,
    )
```

```python
import jax
import jax.numpy as jnp
import numpy as np
from jax import lax
from jax.experimental import pallas as pl
from jax.experimental.pallas import tpu as pltpu
from jax.sharding import Mesh, PartitionSpec as P

ROW, COL = ("x", "core"), ("z", "y")
ALL = ROW + COL
NT = (((1,), (1,)), ((), ()))
RING = {s: [(i, (i + s) % 4) for i in range(4)] for s in (1, 2, 3)}
SWAP = [(0, 1), (1, 0)]
LOCAL = pl.BlockSpec(memory_space=pltpu.VMEM)


def both_cores(pieces):
    return pieces + [lax.ppermute(piece, "core", SWAP) for piece in pieces]


def row_gather(block):
    return both_cores([block] + [lax.ppermute(block, "x", RING[s]) for s in (1, 2, 3)])


def row_gather_beside(block, beside):
    pieces = [block] + [lax.ppermute(block, "x", RING[s]) for s in (1, 2, 3)]
    own, beside = lax.optimization_barrier((block, beside))
    return pieces + [lax.ppermute(piece, "core", SWAP) for piece in [own] + pieces[1:]], beside


def turned(s):
    pairs = []
    for a in range(4):
        for core in range(2):
            for b in range(4):
                for y in range(4):
                    source = ((a * 2 + core) * 4 + b) * 4 + y
                    target = ((((b - s) % 4) * 2 + core) * 4 + a) * 4 + y
                    pairs.append((source, target))
    return pairs


def slab_gather(block):
    return both_cores([lax.ppermute(block, ALL, turned(s)) for s in range(4)])


def y_gather(blocks):
    return [blocks] + [lax.ppermute(blocks, "y", RING[s]) for s in (1, 2, 3)]


def z_sum(parts):
    total = parts[0]
    for t in (1, 2, 3):
        total = total + lax.ppermute(parts[t], "z", RING[t])
    return total


def split(v):
    high = v.astype(jnp.bfloat16)
    return high, (v - high.astype(jnp.float32)).astype(jnp.bfloat16)


def three(v, doubled):
    high, low = split(v)
    return jnp.concatenate([high, high, low] if doubled else [high, low, high], axis=1)


def in_vmem(shape, dtype=jnp.float32):
    return pltpu.VMEM(shape, dtype)


def local_call(kernel, operands, shapes, scratch, name, flops):
    nbytes = 4 * sum(int(np.prod(v.shape)) for v in operands)
    return pl.pallas_call(
        kernel,
        out_shape=shapes,
        in_specs=[LOCAL] * len(operands),
        out_specs=[LOCAL] * len(shapes) if isinstance(shapes, list) else LOCAL,
        scratch_shapes=scratch,
        compiler_params=pltpu.CompilerParams(vmem_limit_bytes=16 * 1024 * 1024),
        cost_estimate=pl.CostEstimate(flops=flops, bytes_accessed=nbytes, transcendentals=0),
        name=name,
    )(*[pltpu.with_memory_space_constraint(v, pltpu.VMEM) for v in operands])


def fetch(blocks, index):
    def kernel(blocks_ref, out, sems):
        copies = []
        for i in range(4):
            part = pl.ds(4 * i, 4)
            copies.append(pltpu.make_async_copy(blocks_ref.at[part, index], out.at[part], sems.at[i]))
        for copy in copies:
            copy.start()
        for copy in copies:
            copy.wait()

    return pl.pallas_call(
        kernel,
        out_shape=in_vmem((16, 256, 128)),
        in_specs=[pl.BlockSpec(memory_space=pl.ANY)],
        out_specs=LOCAL,
        scratch_shapes=[pltpu.SemaphoreType.DMA((4,))],
        compiler_params=pltpu.CompilerParams(vmem_limit_bytes=8 * 1024 * 1024),
        cost_estimate=pl.CostEstimate(flops=0, bytes_accessed=4194304, transcendentals=0),
        name="fetch",
    )(pltpu.with_memory_space_constraint(blocks, pltpu.HBM))


def slab_product(factor, indices, gathered):
    n = len(indices)

    def kernel(*refs):
        f, pieces, out, (chunks, blocks) = refs[:4], refs[4:12], refs[12:16], refs[16:]
        x, z, y, core = (lax.axis_index(name) for name in ("x", "z", "y", "core"))
        for side, which in ((0, core), (4, 1 - core)):
            for h in range(2):
                for s in range(4):
                    chunks[which * 2 + h, s * 64 : s * 64 + 64] = pieces[side + s][:, h * 128 : h * 128 + 128]
        for at, index in enumerate(indices):
            value = jnp.zeros((256, 256), jnp.float32)
            for k in (0, 2):
                rows = jnp.concatenate([chunks[lax.rem(y - k - h + 4, 4)] for h in (0, 1)], axis=1)
                block = jnp.concatenate([f[k][index], f[k + 1][index]], axis=1)
                value += lax.dot_general(three(rows, False), three(block, True), NT, preferred_element_type=jnp.float32)
            blocks[at] = value.reshape(4, 64, 256)
        for t in range(4):
            for at in range(n):
                out[t][at] = blocks[at, lax.rem(t + z - x + 4, 4)]

    return local_call(
        kernel,
        [*factor, *gathered],
        [in_vmem((n, 64, 256))] * 4,
        [pltpu.VMEM((4, 256, 128), jnp.float32), pltpu.VMEM((n, 4, 64, 256), jnp.float32)],
        "slab_product",
        n * 2 * 3 * 256 * 256 * 512,
    )


def by_row(pieces):
    x, core = lax.axis_index("x"), lax.axis_index("core")
    for side, which in ((0, core), (4, 1 - core)):
        for k in range(4):
            yield lax.rem(x - k + 4, 4) * 2 + which, pieces[side + k]


def full_product(base, terms):
    n = len(terms)

    def kernel(*refs):
        scratch = refs[len(refs) - n :]
        out = refs[len(refs) - n - 1]
        both = jnp.zeros((128, 256), jnp.float32)
        cross = jnp.zeros((64, 256), jnp.float32)
        for term, chunks in enumerate(scratch):
            f, pieces = refs[9 * term], refs[9 * term + 1 : 9 * term + 9]
            for row, piece in by_row(pieces):
                chunks[row, :64], chunks[row, 64:] = split(piece[...])
            for q in range(8):
                high, low = split(jnp.concatenate([f[2 * q], f[2 * q + 1]], axis=1))
                rows = chunks[q]
                both += lax.dot_general(rows, high, NT, preferred_element_type=jnp.float32)
                cross += lax.dot_general(rows[:64], low, NT, preferred_element_type=jnp.float32)
        total = both[:64] + both[64:] + cross
        out[...] = total if base is None else refs[9 * n][...] - total

    operands = [v for block, gathered in terms for v in (block, *gathered)]
    return local_call(
        kernel,
        operands + ([] if base is None else [base]),
        in_vmem((64, 256)),
        [pltpu.VMEM((8, 128, 256), jnp.bfloat16)] * n,
        "full_product",
        n * 2 * 3 * 64 * 256 * 2048,
    )


def spread_to(turn):
    return [(r * 16 + 2 * q + b, q * 16 + 2 * r + (b + turn) % 2) for r in range(8) for q in range(8) for b in range(2)]


def spread(blocks):
    odd = lax.axis_index("y") % 2 == 1
    low, high = blocks[:, :, :128], blocks[:, :, 128:]
    same = lax.ppermute(jnp.where(odd, high, low), ALL, spread_to(0))
    cross = lax.ppermute(jnp.where(odd, low, high), ALL, spread_to(1))
    return row_gather(jnp.concatenate([jnp.where(odd, cross, same), jnp.where(odd, same, cross)], axis=1))


def split_rows(gathered):
    n = gathered[0].shape[0]

    def kernel(*refs):
        out = refs[-1]
        for row, piece in by_row(refs[:8]):
            at = pl.ds(pl.multiple_of(row * 128, 128), 128)
            for j in range(n):
                one, two = split(piece[j])
                out[at, j * 128 : j * 128 + 128] = one
                out[at, (n + j) * 128 : (n + j + 1) * 128] = two

    return local_call(kernel, gathered, in_vmem((1024, 2 * n * 128), jnp.bfloat16), [], "split_rows", 0)


def trailing_product(factor, early, last):
    def kernel(f, early, last, out, rows):
        @pl.when(pl.program_id(0) == 0)
        def _():
            for part, side in enumerate((0, 1, 0)):
                rows[:, part * 512 : part * 512 + 384] = early[:, side * 384 : side * 384 + 384]
                rows[:, part * 512 + 384 : part * 512 + 512] = last[:, side * 128 : side * 128 + 128]

        for t in range(2):
            block = jnp.concatenate([f[t, pl.ds(j, 256, stride=4), :] for j in range(4)], axis=1)
            value = lax.dot_general(rows[...], three(block, True), NT, preferred_element_type=jnp.float32)
            out[:, t] = value.reshape(16, 64, 256)

    return pl.pallas_call(
        kernel,
        grid=(6,),
        out_shape=jax.ShapeDtypeStruct((16, 12, 64, 256), jnp.float32),
        in_specs=[
            pl.BlockSpec((2, 1024, 128), lambda t: (t, 0, 0)),
            pl.BlockSpec((1024, 768), lambda t: (0, 0)),
            pl.BlockSpec((1024, 256), lambda t: (0, 0)),
        ],
        out_specs=pl.BlockSpec((16, 2, 64, 256), lambda t: (0, t, 0, 0)),
        scratch_shapes=[pltpu.VMEM((1024, 1536), jnp.bfloat16)],
        compiler_params=pltpu.CompilerParams(vmem_limit_bytes=56 * 1024 * 1024),
        cost_estimate=pl.CostEstimate(flops=2 * 3 * 1024 * 3072 * 512, bytes_accessed=20971520, transcendentals=0),
        name="trailing_product",
    )(factor, early, last)


def shards(panel, inverse_blocks, trailing_factor, columns, trailing_columns):
    columns_t = jnp.transpose(columns, (0, 2, 1))
    group = y_gather(inverse_blocks[0:1])
    below = y_gather(jnp.concatenate([panel[0:2], panel[3:4]]))
    near = lax.all_gather(jnp.concatenate([inverse_blocks[1:2], panel[2:3], inverse_blocks[2:3]]), COL, axis=0)
    far = lax.all_gather(jnp.concatenate([panel[4:6], inverse_blocks[3:4]]), COL, axis=0)

    first = z_sum(slab_product(group, (0,), slab_gather(columns_t[0])))[0]
    bases = columns_t[1:4] - z_sum(slab_product(below, (0, 1, 2), slab_gather(first)))
    second = full_product(None, [(fetch(near, 0), row_gather(bases[0]))])
    gathered_second, block = row_gather_beside(second, fetch(near, 1))
    reduced = full_product(bases[1], [(block, gathered_second)])
    gathered, block = row_gather_beside(reduced, fetch(near, 2))
    third = full_product(None, [(block, gathered)])
    gathered = row_gather(third)
    (first, second, third), gathered = lax.optimization_barrier(((first, second, third), gathered))
    early = spread(jnp.stack([first, second, third]))
    early, far = lax.optimization_barrier((early, far))
    reduced = full_product(bases[2], [(fetch(far, 0), gathered_second), (fetch(far, 1), gathered)])
    gathered, (block, early) = row_gather_beside(reduced, (fetch(far, 2), split_rows(early)))
    fourth = full_product(None, [(block, gathered)])

    partial = trailing_product(trailing_factor.reshape(12, 1024, 128), early, split_rows(spread(fourth[None])))
    updated = jnp.transpose(trailing_columns, (0, 2, 1)) - lax.psum_scatter(partial, COL, scatter_dimension=0)

    whitened_t = jnp.stack([first, second, third, fourth])
    local_squares = jnp.sum(whitened_t * whitened_t, axis=(0, 2))
    variance_drop = lax.psum(local_squares, ROW) / 8192
    return (jnp.transpose(whitened_t, (0, 2, 1)), jnp.transpose(updated, (0, 2, 1)), variance_drop)


def solution(mesh):
    mesh = Mesh(np.asarray(mesh.devices).reshape(4, 2, 4, 4), ("x", "core", "z", "y"))
    return jax.shard_map(
        shards,
        mesh=mesh,
        in_specs=(
            P(None, ROW, COL),
            P(None, ROW, COL),
            P(None, ROW, None, COL),
            P(None, ROW, COL),
            P(None, ROW, COL),
        ),
        out_specs=(P(None, ROW, COL), P(None, ROW, COL), P(COL)),
        check_vma=False,
    )
```
